256 devices in a mesh: row: 16 (over y, z_lo, core), col: 16 (over z_hi, x).
Axes of the slice: x: 4, y: 4, z: 8 (z_hi: 4, z_lo: 2; z = z_hi * 2 + z_lo), core: 2. Of those that a mesh axis runs over, the one named last changes fastest.
Arguments:
- gradient: bfloat16 [1024, 25600], P('row', 'col'), may hold values from -6 to 6
- basis: bfloat16 [25600, 25600], P('col', 'row'), may hold values from -0.0390625 to 0.0390625
- moment: float32 [1024, 25600], P('col', 'row'), may hold values from -2 to 2
- second: float32 [1024, 25600], P('col', 'row'), may hold values from 0.05 to 2
Outputs:
- new_moment: float32 [1024, 25600], P('col', 'row')
- new_second: float32 [1024, 25600], P('col', 'row')
- direction: bfloat16 [1024, 25600], P('row', 'col')
The draws below stay inside these ranges and needn't reach their ends.
All inputs are finite; a program needn't handle non-finite values.
Results may differ from the reference program's by a relative error of at most 0.0048.
Values may be sent and summed in bfloat16 or wider, within the bound.
A program may use at most 64 MiB of HBM per device.

```python
import math
import jax
import jax.numpy as jnp
from jax import lax

N = 25600
ROWS = 1024


def level_of(rng, dims, pieces, low, largest):
    loudness, own = 1.0, jax.random.fold_in(rng, 6)
    for dim, blocks in pieces:
        heights = jnp.exp(jax.random.uniform(jax.random.fold_in(own, dim), (blocks,), jnp.float32, low / len(pieces), largest / len(pieces)))
        loudness = loudness * jnp.repeat(heights, dims[dim] // blocks).reshape([-1 if axis == dim else 1 for axis in range(len(dims))])
    return loudness


def scatter_about(rng, extent, deviation, most, split=(), dtype=jnp.bfloat16):
    entries = deviation * jax.random.normal(rng, extent, jnp.float32)
    if split:
        entries = entries * level_of(rng, extent, split, -0.22, 0.18)
    return jnp.clip(entries, -most, most).astype(dtype)


def setup_inputs(seed: int = 0) -> dict:
    key_of = jax.random.split(jax.random.key(seed), 5)
    return {
        "gradient": scatter_about(key_of[0], (ROWS, N), 1.0, 6.0, ((0, 16), (1, 16))),
        "basis": scatter_about(key_of[1], (N, N), N ** -0.5, 0.0390625, ((0, 16), (1, 16))),
        "moment": scatter_about(key_of[2], (ROWS, N), 0.3, 2.0, ((0, 16), (1, 16)), jnp.float32),
        "second": jnp.clip(jnp.exp(math.log(2.0) - 3.6888794 * jax.random.uniform(key_of[3], (ROWS, N), jnp.float32) ** level_of(key_of[3], (ROWS, N), ((0, 16), (1, 16)), -0.2, 0.2)), 0.05, 2.0),
    }


beta_one = 0.9
beta_two = 0.95
bias_one = 1.0 - 0.9 ** 10
bias_two = 1.0 - 0.95 ** 10
epsilon = 1e-08

def reference(gradient, basis, moment, second):
    rotated = jnp.dot(gradient, basis, preferred_element_type=jnp.float32)
    new_moment = beta_one * moment + (1.0 - beta_one) * rotated
    new_second = beta_two * second + (1.0 - beta_two) * rotated * rotated
    scaled = (new_moment / bias_one / (jnp.sqrt(new_second / bias_two) + epsilon)).astype(jnp.bfloat16)
    direction = lax.dot_general(scaled, basis, (((1,), (1,)), ((), ())), preferred_element_type=jnp.float32)
    return (new_moment, new_second, direction.astype(jnp.bfloat16))
```

```python
import functools

import jax
import jax.numpy as jnp
from jax import lax
from jax.experimental import pallas as pl
from jax.experimental.pallas import tpu as pltpu
from jax.sharding import PartitionSpec as P

MESH = pl.DeviceIdType.MESH
F32, BF16 = jnp.float32, jnp.bfloat16

beta_one = 0.9
beta_two = 0.95
bias_one = 1.0 - 0.9**10
bias_two = 1.0 - 0.95**10
epsilon = 1e-08

N = 1600
Q = 4
T = 16
TILES = [(j, min(256, N - j)) for j in range(0, N, 256)]

KINDS = ("g", "cf", "A", "B", "C", "D", "E1", "E2", "F", "G", "H", "I")
ROWS = dict(g=112, cf=128, A=64, B=128, C=48, D=48, E1=64, E2=64, F=64, G=128, H=96, I=16)

ORDER = [(0, 'g'), (1, 'g'), (0, 'cf'), (2, 'g'), (0, 'm1'), (3, 'g'), (1, 'cf'), (0, 'a'), (1, 'm1'), (2, 'cf'),
         (3, 'cf'), (0, 'b'), (1, 'a'), (2, 'm1'), (1, 'b'), (2, 'a'), (0, 'ad'), (3, 'm1'), (1, 'ad'), (3, 'a'),
         (0, 'e'), (2, 'b'), (3, 'b'), (1, 'e'), (0, 'f'), (2, 'ad'), (1, 'f'), (0, 'm2'), (3, 'ad'), (1, 'm2'),
         (2, 'e'), (0, 'h'), (2, 'f'), (1, 'h'), (3, 'e'), (2, 'm2'), (3, 'f'), (0, 'i'), (2, 'h'), (1, 'i'),
         (3, 'm2'), (3, 'h'), (2, 'i'), (3, 'i'), (1, 'o'), (0, 'o'), (2, 'o'), (3, 'o')]


def kernel(
    grad, basis, moment, second, new_moment, new_second, direction,
    bv, mv, sv, nmv, nsv, dv,
    gath, part, part16, a_in, b_out, b_in, c_out, c_own, c_in, step, g_in, h_out, h_own, h_in, i_own, i_out, i_in,
    send, recv, local,
):
    row, col = lax.axis_index("row"), lax.axis_index("col")
    core, zlo, y = row % 2, (row // 2) % 2, row // 4
    x, zhi = col % 4, col // 4

    def at_row(yy, zz, cc):
        return ((yy * 2 + zz) * 2 + cc, col)

    def at_col(zz, xx):
        return (row, zz * 4 + xx)

    x_up, x_down, x_far = (x + 1) % 4, (x + 3) % 4, (x + 2) % 4
    right, left = at_col(zhi, x_up), at_col(zhi, x_down)
    sibling = at_row(y, zlo, 1 - core)
    partner = at_row(y, 1 - zlo, core)
    peers_z = [at_col((zhi + d) % 4, x) for d in (1, 2, 3)]
    peers_y = [at_row((y + d) % 4, zlo, core) for d in (1, 2, 3)]
    peers_row = [partner] + [at_row((y + d) % 4, z, core) for d in (1, 2, 3) for z in (0, 1)]

    def ds(start, size):
        return pl.ds(pl.multiple_of(start, 16), size)

    mine = ((zlo * 2 + core) * 4 + y) * T
    own = [
        pltpu.make_async_copy(grad.at[pl.ds(q * T, T)], gath.at[q, ds(mine, T)], local.at[q]) for q in range(Q)
    ]
    for c in own:
        c.start()
    load_b = pltpu.make_async_copy(basis, bv, local.at[4])
    load_m = pltpu.make_async_copy(moment, mv, local.at[5])
    load_s = pltpu.make_async_copy(second, sv, local.at[6])
    load_b.start()
    load_m.start()
    load_s.start()

    barrier = pltpu.get_barrier_semaphore()
    partners = [right, left, sibling] + peers_z + peers_row
    for d in partners:
        pl.semaphore_signal(barrier, inc=1, device_id=d, device_id_type=MESH)
    pl.semaphore_wait(barrier, len(partners))

    def put(kind, q, src, dst, to):
        k = KINDS.index(kind)
        pltpu.make_async_remote_copy(
            src_ref=src, dst_ref=dst, send_sem=send.at[k, q], recv_sem=recv.at[k, q], device_id=to, device_id_type=MESH
        ).start()

    def span(kind):
        ref = g_in if kind == "G" else part16
        return ref.at[0, pl.ds(0, ROWS[kind])]

    def got(kind, q):
        pltpu.make_async_copy(span(kind), span(kind), recv.at[KINDS.index(kind), q]).wait()

    def sent(kind, q):
        pltpu.make_async_copy(span(kind), span(kind), send.at[KINDS.index(kind), q]).wait()

    def gather(q):
        own[q].wait()
        for d in peers_row:
            block = gath.at[q, ds(mine, T)]
            put("g", q, block, block, d)

    def gather_core(q):
        got("g", q)
        for z in (0, 1):
            block = gath.at[q, ds((z * 2 + core) * 64, 64)]
            put("cf", q, block, block, sibling)

    def forward(q):
        got("cf", q)
        if q == 0:
            load_b.wait()
        for j, w in TILES:
            p = jnp.dot(gath[q], bv[:, j : j + w], preferred_element_type=F32)
            part[q, :, j : j + w] = p
            part16[q, :, j : j + w] = p.astype(BF16)
        put("A", q, part16.at[q, ds(x_far * 64, 32)], a_in.at[q, pl.ds(0, 32)], right)
        put("A", q, part16.at[q, ds(x_far * 64 + 32, 32)], a_in.at[q, pl.ds(32, 32)], left)
        put("B", q, part16.at[q, ds(x_up * 64 + 32, 32)], b_in.at[q, pl.ds(32, 32)], right)
        put("B", q, part16.at[q, ds(x_down * 64, 32)], b_in.at[q, pl.ds(64, 32)], left)

    def add_far(q):
        got("A", q)
        for half, start in ((0, x_up * 64), (1, x_down * 64 + 32)):
            for i in range(0, 32, T):
                at = half * 32 + i
                b_out[q, at : at + T] = (
                    part[q, ds(start + i, T)] + a_in[q, at : at + T].astype(F32)
                ).astype(BF16)
        put("B", q, b_out.at[q, pl.ds(0, 32)], b_in.at[q, pl.ds(0, 32)], right)
        put("B", q, b_out.at[q, pl.ds(32, 32)], b_in.at[q, pl.ds(96, 32)], left)

    def sum_x(q, i):
        return (
            part[q, ds(x * 64 + i, T)]
            + b_in[q, ds(i, T)].astype(F32)
            + b_in[q, ds(64 + i, T)].astype(F32)
        )

    def add_x(q):
        got("B", q)
        for i in range(0, 64, T):
            c_out[q, i : i + T] = sum_x(q, i).astype(BF16)
        for d in (1, 2, 3):
            put("C", q, c_out.at[q, ds((zhi + d) % 4 * T, T)], c_in.at[q, pl.ds((d - 1) * T, T)], peers_z[d - 1])
        c_own[q] = sum_x(q, zhi * T)

    def adam(q):
        if q == 0:
            load_m.wait()
            load_s.wait()
        got("C", q)
        rotated = c_own[q]
        for d in range(3):
            rotated += c_in[q, d * T : d * T + T].astype(F32)
        rows = slice(q * T, q * T + T)
        nm = beta_one * mv[rows] + (1.0 - beta_one) * rotated
        ns = beta_two * sv[rows] + (1.0 - beta_two) * rotated * rotated
        nmv[rows] = nm
        nsv[rows] = ns
        block = step.at[q, ds(x * 64 + zhi * T, T)]
        block[...] = (nm / bias_one / (jnp.sqrt(ns / bias_two) + epsilon)).astype(BF16)
        for d in peers_z:
            put("D", q, block, block, d)

    def spread(q):
        got("D", q)
        first, last = (step.at[q, ds(x * 64 + i, 32)] for i in (0, 32))
        put("E1", q, first, first, right)
        put("E1", q, last, last, left)
        put("E2", q, last, last, right)
        put("E2", q, first, first, left)

    def spread_far(q):
        got("E1", q)
        first, last = step.at[q, ds(x_down * 64, 32)], step.at[q, ds(x_up * 64 + 32, 32)]
        put("F", q, first, first, right)
        put("F", q, last, last, left)

    def back(q):
        got("E2", q)
        got("F", q)
        for j, w in TILES:
            part[q, :, j : j + w] = lax.dot_general(
                step[q], bv[j : j + w, :], (((1,), (1,)), ((), ())), preferred_element_type=F32
            )
        for z in (0, 1):
            put("G", q, part.at[q, ds((z * 2 + 1 - core) * 64, 64)], g_in.at[q, pl.ds(z * 64, 64)], sibling)

    def add_core(q):
        got("G", q)

        def total(z, yy):
            return part[q, ds((z * 2 + core) * 64 + yy * T, T)] + g_in[q, ds(z * 64 + yy * T, T)]

        for yy in range(4):
            for z in (0, 1):
                at = (yy * 2 + z) * T
                h_out[q, at : at + T] = total(z, yy).astype(BF16)
        for d in (1, 2, 3):
            put("H", q, h_out.at[q, ds((y + d) % 4 * 32, 32)], h_in.at[q, pl.ds((d - 1) * 32, 32)], peers_y[d - 1])
        for z in (0, 1):
            h_own[q, z * T : z * T + T] = total(z, y)

    def add_y(q):
        got("H", q)

        def total(z):
            t = h_own[q, ds(z * T, T)]
            for d in range(3):
                t += h_in[q, ds(d * 32 + z * T, T)].astype(F32)
            return t

        i_out[q] = total(1 - zlo).astype(BF16)
        put("I", q, i_out.at[q], i_in.at[q], partner)
        i_own[q] = total(zlo)

    def finish(q):
        got("I", q)
        dv[q * T : q * T + T] = (i_own[q] + i_in[q].astype(F32)).astype(BF16)

    phases = dict(
        g=gather, cf=gather_core, m1=forward, a=add_far, b=add_x, ad=adam, e=spread, f=spread_far, m2=back, h=add_core,
        i=add_y, o=finish,
    )
    moments = [
        pltpu.make_async_copy(nmv, new_moment, local.at[7]),
        pltpu.make_async_copy(nsv, new_second, local.at[8]),
    ]
    left_over = set(range(Q))
    for q, name in ORDER:
        phases[name](q)
        if name == "ad":
            left_over.remove(q)
            if not left_over:
                for c in moments:
                    c.start()
    out = pltpu.make_async_copy(dv, direction, local.at[9])
    out.start()
    for q in range(Q):
        for kind in KINDS:
            sent(kind, q)
    for c in moments:
        c.wait()
    out.wait()


def on_device(gradient, basis, moment, second):
    def vm(rows, dtype=BF16):
        return pltpu.VMEM((Q, rows, N), dtype)

    small = [pltpu.VMEM((Q * T, N), F32)] * 4 + [pltpu.VMEM((Q * T, N), BF16)]
    anywhere = pl.BlockSpec(memory_space=pl.ANY)
    return pl.pallas_call(
        kernel,
        out_shape=[
            jax.ShapeDtypeStruct((Q * T, N), F32),
            jax.ShapeDtypeStruct((Q * T, N), F32),
            jax.ShapeDtypeStruct((Q * T, N), BF16),
        ],
        in_specs=[anywhere] * 4,
        out_specs=[anywhere] * 3,
        scratch_shapes=[pltpu.VMEM((N, N), BF16)] + small + [
            vm(256), vm(256, F32), vm(256), vm(64), vm(64), vm(128), vm(64), vm(T, F32), vm(48), vm(256),
            vm(128, F32), vm(128), vm(32, F32), vm(96), vm(T, F32), vm(T), vm(T),
            pltpu.SemaphoreType.DMA((len(KINDS), Q)),
            pltpu.SemaphoreType.DMA((len(KINDS), Q)),
            pltpu.SemaphoreType.DMA((10,)),
        ],
        compiler_params=pltpu.CompilerParams(
            collective_id=0, has_side_effects=True, vmem_limit_bytes=58 * 1024 * 1024
        ),
        cost_estimate=pl.CostEstimate(flops=4 * 1024 * N * N, bytes_accessed=8 << 20, transcendentals=0),
        name="soap_step",
    )(gradient, basis, moment, second)


def solution(mesh):
    return jax.shard_map(
        on_device,
        mesh=mesh,
        in_specs=(P("row", "col"), P("col", "row"), P("col", "row"), P("col", "row")),
        out_specs=(P("col", "row"), P("col", "row"), P("row", "col")),
        check_vma=False,
    )
```

```python
import jax
import jax.numpy as jnp
from jax import lax
from jax.experimental import pallas as pl
from jax.experimental.pallas import tpu as pltpu
from jax.sharding import PartitionSpec as P

MESH = pl.DeviceIdType.MESH
F32, BF16 = jnp.float32, jnp.bfloat16

beta_one = 0.9
beta_two = 0.95
bias_one = 1.0 - 0.9**10
bias_two = 1.0 - 0.95**10
epsilon = 1e-08

N = 1600
Q = 4
T = 16
SPLIT = [(0, 768), (768, 832)]
J = len(SPLIT)


def tiles(start, size):
    return [(j, min(256, start + size - j)) for j in range(start, start + size, 256)]


ROWS = dict(g=112, cf=128, A=64, B=128, C=48, D=48, E1=64, E2=64, F=64, G=128, H=112)
KINDS = tuple(ROWS)
WHOLE = ("g", "cf", "G", "H")


ORDER = [
    (0, "g", 0), (1, "g", 0), (2, "g", 0), (0, "cf", 0), (3, "g", 0), (0, "m1", 0), (0, "m1", 1), (1, "cf", 0),
    (0, "a", 0), (1, "m1", 0), (0, "a", 1), (0, "b", 0), (2, "cf", 0), (1, "a", 0), (1, "m1", 1), (0, "b", 1),
    (3, "cf", 0), (2, "m1", 0), (1, "b", 0), (1, "a", 1), (3, "m1", 0), (0, "ad", 0), (3, "m1", 1), (0, "ad", 1),
    (1, "ad", 0), (3, "a", 0), (2, "a", 0), (1, "b", 1), (2, "m1", 1), (3, "b", 0), (3, "a", 1), (0, "e", 0),
    (2, "b", 0), (2, "a", 1), (3, "b", 1), (1, "e", 0), (1, "ad", 1), (0, "e", 1), (1, "f", 0), (3, "ad", 0),
    (2, "b", 1), (0, "f", 0), (0, "f", 1), (2, "ad", 0), (1, "e", 1), (3, "e", 0), (0, "m2", 0), (3, "ad", 1),
    (1, "m2", 0), (1, "f", 1), (0, "m2", 1), (3, "f", 0), (2, "ad", 1), (2, "e", 0), (0, "h", 1), (3, "e", 1),
    (1, "m2", 1), (3, "m2a", 0), (2, "f", 0), (2, "e", 1), (1, "h", 1), (3, "f", 1), (3, "m2b", 0), (3, "m2a", 1),
    (2, "m2", 0), (2, "f", 1), (3, "ha", 1), (3, "m2b", 1), (2, "m2", 1), (3, "hb", 1), (1, "o", 1), (0, "o", 1),
    (2, "h", 1), (3, "o", 1), (2, "o", 1),
]


def kernel(
    grad, basis, moment, second, nmv, nsv, dv,
    bv, mv, sv, gath, part, part16, a_in, b_out, b_in, c_out, c_own, c_in, step, g_in, h_out, h_own, h_in,
    send, recv, recv_g, local,
):
    row, col = lax.axis_index("row"), lax.axis_index("col")
    core, zlo, y = row % 2, (row // 2) % 2, row // 4
    x, zhi = col % 4, col // 4

    def at_row(yy, zz, cc):
        return ((yy * 2 + zz) * 2 + cc, col)

    def at_col(zz, xx):
        return (row, zz * 4 + xx)

    x_up, x_down, x_far = (x + 1) % 4, (x + 3) % 4, (x + 2) % 4
    right, left = at_col(zhi, x_up), at_col(zhi, x_down)
    sibling = at_row(y, zlo, 1 - core)
    partner = at_row(y, 1 - zlo, core)
    peers_z = [at_col((zhi + d) % 4, x) for d in (1, 2, 3)]
    peers_row = [partner] + [at_row((y + d) % 4, z, core) for d in (1, 2, 3) for z in (0, 1)]

    def ds(start, size):
        return pl.ds(pl.multiple_of(start, 16), size)

    def cols(j):
        return pl.ds(*SPLIT[j])

    mine = ((zlo * 2 + core) * 4 + y) * T
    own = [
        pltpu.make_async_copy(grad.at[pl.ds(q * T, T)], gath.at[q, ds(mine, T)], local.at[q]) for q in range(Q)
    ]
    for c in own:
        c.start()
    load_b = pltpu.make_async_copy(basis, bv, local.at[4])
    load_m = pltpu.make_async_copy(moment, mv, local.at[5])
    load_s = pltpu.make_async_copy(second, sv, local.at[6])
    load_b.start()
    load_m.start()
    load_s.start()

    barrier = pltpu.get_barrier_semaphore()
    partners = [right, left, sibling] + peers_z + peers_row
    for d in partners:
        pl.semaphore_signal(barrier, inc=1, device_id=d, device_id_type=MESH)
    pl.semaphore_wait(barrier, len(partners))

    def put(kind, sem, src, dst, to):
        pltpu.make_async_remote_copy(
            src_ref=src, dst_ref=dst, send_sem=send.at[KINDS.index(kind)], recv_sem=sem, device_id=to,
            device_id_type=MESH,
        ).start()

    def arrival(kind, q, j=0):
        return recv.at[KINDS.index(kind), q, j]

    def await_rows(sem, ref):
        pltpu.make_async_copy(ref, ref, sem).wait()

    def got(kind, q, j=0):
        span = part16.at[0, pl.ds(0, ROWS[kind])]
        if kind not in WHOLE:
            span = part16.at[0, pl.ds(0, ROWS[kind]), cols(j)]
        await_rows(arrival(kind, q, j), span)

    def sent(kind):
        ref = part if kind == "G" else part16
        await_rows(send.at[KINDS.index(kind)], ref.at[:, pl.ds(0, ROWS[kind])])

    def gather(q, j):
        own[q].wait()
        for d in peers_row:
            block = gath.at[q, ds(mine, T)]
            put("g", arrival("g", q), block, block, d)

    def gather_core(q, j):
        got("g", q)
        for z in (0, 1):
            block = gath.at[q, ds((z * 2 + core) * 64, 64)]
            put("cf", arrival("cf", q), block, block, sibling)

    def forward(q, j):
        if j == 0:
            got("cf", q)
            if q == 0:
                load_b.wait()
        for s, w in tiles(*SPLIT[j]):
            p = jnp.dot(gath[q], bv[:, s : s + w], preferred_element_type=F32)
            part[q, :, s : s + w] = p
            part16[q, :, s : s + w] = p.astype(BF16)
        c = cols(j)
        for kind, block, ref, at, to in (
            ("A", x_far * 64, a_in, 0, right),
            ("A", x_far * 64 + 32, a_in, 32, left),
            ("B", x_up * 64 + 32, b_in, 32, right),
            ("B", x_down * 64, b_in, 64, left),
        ):
            put(kind, arrival(kind, q, j), part16.at[q, ds(block, 32), c], ref.at[q, pl.ds(at, 32), c], to)

    def add_far(q, j):
        got("A", q, j)
        c = cols(j)
        for half, start in ((0, x_up * 64), (1, x_down * 64 + 32)):
            for i in range(0, 32, T):
                at = half * 32 + i
                b_out[q, at : at + T, c] = (
                    part[q, ds(start + i, T), c] + a_in[q, at : at + T, c].astype(F32)
                ).astype(BF16)
        put("B", arrival("B", q, j), b_out.at[q, pl.ds(0, 32), c], b_in.at[q, pl.ds(0, 32), c], right)
        put("B", arrival("B", q, j), b_out.at[q, pl.ds(32, 32), c], b_in.at[q, pl.ds(96, 32), c], left)

    def add_x(q, j):
        got("B", q, j)
        c = cols(j)

        def total(i):
            return (
                part[q, ds(x * 64 + i, T), c] + b_in[q, ds(i, T), c].astype(F32) + b_in[q, ds(64 + i, T), c].astype(F32)
            )

        for i in range(0, 64, T):
            c_out[q, i : i + T, c] = total(i).astype(BF16)
        for d in (1, 2, 3):
            put(
                "C", arrival("C", q, j), c_out.at[q, ds((zhi + d) % 4 * T, T), c],
                c_in.at[q, pl.ds((d - 1) * T, T), c], peers_z[d - 1],
            )
        c_own[q, :, c] = total(zhi * T)

    def adam(q, j):
        if q == 0 and j == 0:
            load_m.wait()
            load_s.wait()
        got("C", q, j)
        c = cols(j)
        rotated = c_own[q, :, c]
        for d in range(3):
            rotated += c_in[q, d * T : d * T + T, c].astype(F32)
        rows = pl.ds(q * T, T)
        nm = beta_one * mv[rows, c] + (1.0 - beta_one) * rotated
        ns = beta_two * sv[rows, c] + (1.0 - beta_two) * rotated * rotated
        nmv[rows, c] = nm
        nsv[rows, c] = ns
        block = step.at[q, ds(64 + zhi * T, T), c]
        block[...] = (nm / bias_one / (jnp.sqrt(ns / bias_two) + epsilon)).astype(BF16)
        for d in peers_z:
            put("D", arrival("D", q, j), block, block, d)

    def rows_of(q, j, start):
        return step.at[q, pl.ds(start, 32), cols(j)]

    def spread(q, j):
        got("D", q, j)
        put("E1", arrival("E1", q, j), rows_of(q, j, 64), rows_of(q, j, 0), right)
        put("E1", arrival("E1", q, j), rows_of(q, j, 96), rows_of(q, j, 160), left)
        put("E2", arrival("E2", q, j), rows_of(q, j, 96), rows_of(q, j, 32), right)
        put("E2", arrival("E2", q, j), rows_of(q, j, 64), rows_of(q, j, 128), left)

    def spread_far(q, j):
        got("E1", q, j)
        put("F", arrival("F", q, j), rows_of(q, j, 0), rows_of(q, j, 192), right)
        put("F", arrival("F", q, j), rows_of(q, j, 160), rows_of(q, j, 224), left)

    def back(q, j, first, size):
        rows = pl.ds(first, size)
        for s, w in tiles(0, N):
            d = lax.dot_general(
                step[q, rows, cols(j)], bv[s : s + w, cols(j)], (((1,), (1,)), ((), ())), preferred_element_type=F32
            )
            if j:
                d += part[q, rows, s : s + w]
            part[q, rows, s : s + w] = d

    def slot(dest):
        return (dest - x + 5) % 4 * 64

    def give_core(q, z):
        put(
            "G", recv_g.at[q, z], part.at[q, ds(slot(z * 2 + 1 - core), 64)], g_in.at[q, pl.ds(z * 64, 64)], sibling
        )

    def add_core(q, z):
        await_rows(recv_g.at[q, z], g_in.at[q, pl.ds(0, 64)])

        def total(yy):
            return part[q, ds(slot(z * 2 + core) + yy * T, T)] + g_in[q, ds(z * 64 + yy * T, T)]

        other = (z + zlo) % 2
        for d in range(4):
            yy = (y + d) % 4

            def pass_on(d=d, yy=yy):
                at = z * 64 + d * T
                h_out[q, ds(at, T)] = total(yy).astype(BF16)
                put(
                    "H", arrival("H", q), h_out.at[q, ds(at, T)], h_in.at[q, ds(other * 64 + d * T, T)],
                    at_row(yy, z, core),
                )

            if d:
                pass_on()
            else:
                pl.when(other == 1)(pass_on)

                @pl.when(other == 0)
                def _():
                    h_own[q] = total(y)

    def back_all(q, j):
        if j == 0:
            got("E2", q, 0)
            got("F", q, 0)
        else:
            got("E2", q, 1)
            got("F", q, 1)
        back(q, j, 0, 256)
        if j == J - 1:
            for z in (0, 1):
                give_core(q, z)

    def add_all(q, j):
        for z in (0, 1):
            add_core(q, z)

    def back_near(q, j):
        got("E2", q, j)
        back(q, j, 0, 192)
        if j == J - 1:
            for z in (0, 1):
                pl.when(z * 2 + 1 - core != x_far)(lambda z=z: give_core(q, z))

    def add_near(q, j):
        for z in (0, 1):
            pl.when(z * 2 + core != x_far)(lambda z=z: add_core(q, z))

    def back_far(q, j):
        got("F", q, j)
        back(q, j, 192, 64)
        if j == J - 1:
            for z in (0, 1):
                pl.when(z * 2 + 1 - core == x_far)(lambda z=z: give_core(q, z))

    def add_rest(q, j):
        for z in (0, 1):
            pl.when(z * 2 + core == x_far)(lambda z=z: add_core(q, z))

    def finish(q, j):
        got("H", q)
        total = h_own[q]
        for i in range(1, 8):
            total += h_in[q, i * T : i * T + T].astype(F32)
        dv[q * T : q * T + T] = total.astype(BF16)

    phases = dict(
        g=gather, cf=gather_core, m1=forward, a=add_far, b=add_x, ad=adam, e=spread, f=spread_far,
        m2=back_all, h=add_all, m2a=back_near, ha=add_near, m2b=back_far, hb=add_rest, o=finish,
    )
    for q, name, j in ORDER:
        phases[name](q, j)
    for kind in KINDS:
        sent(kind)


def flush(a, b, c, out_a, out_b, out_c, sems):
    copies = [
        pltpu.make_async_copy(src, dst, sems.at[i])
        for i, (src, dst) in enumerate(((a, out_a), (b, out_b), (c, out_c)))
    ]
    for copy in copies:
        copy.start()
    for copy in copies:
        copy.wait()


def on_device(gradient, basis, moment, second):
    def vm(rows, dtype=BF16):
        return pltpu.VMEM((Q, rows, N), dtype)

    anywhere = pl.BlockSpec(memory_space=pl.ANY)
    in_vmem = pl.BlockSpec(memory_space=pltpu.VMEM)
    shapes = [((Q * T, N), F32), ((Q * T, N), F32), ((Q * T, N), BF16)]
    results = pl.pallas_call(
        kernel,
        out_shape=[pltpu.VMEM(*s) for s in shapes],
        in_specs=[anywhere] * 4,
        out_specs=[in_vmem] * 3,
        scratch_shapes=[pltpu.VMEM((N, N), BF16)] + [pltpu.VMEM((Q * T, N), F32)] * 2 + [
            vm(256), vm(256, F32), vm(256), vm(64), vm(64), vm(128), vm(64), vm(T, F32), vm(48), vm(256),
            vm(128, F32), vm(128), vm(T, F32), vm(128),
            pltpu.SemaphoreType.DMA((len(KINDS),)),
            pltpu.SemaphoreType.DMA((len(KINDS), Q, J)),
            pltpu.SemaphoreType.DMA((Q, 2)),
            pltpu.SemaphoreType.DMA((7,)),
        ],
        compiler_params=pltpu.CompilerParams(
            collective_id=0, has_side_effects=True, vmem_limit_bytes=56 * 1024 * 1024
        ),
        cost_estimate=pl.CostEstimate(flops=4 * 1024 * N * N, bytes_accessed=8 << 20, transcendentals=0),
        name="soap_step",
    )(gradient, basis, moment, second)
    return pl.pallas_call(
        flush,
        out_shape=[jax.ShapeDtypeStruct(*s) for s in shapes],
        in_specs=[in_vmem] * 3,
        out_specs=[anywhere] * 3,
        scratch_shapes=[pltpu.SemaphoreType.DMA((3,))],
        name="flush",
    )(*results)


def solution(mesh):
    return jax.shard_map(
        on_device,
        mesh=mesh,
        in_specs=(P("row", "col"), P("col", "row"), P("col", "row"), P("col", "row")),
        out_specs=(P("col", "row"), P("col", "row"), P("row", "col")),
        check_vma=False,
    )
```

```python
import jax
import jax.numpy as jnp
from jax import lax
from jax.experimental import pallas as pl
from jax.experimental.pallas import tpu as pltpu
from jax.sharding import PartitionSpec as P

MESH = pl.DeviceIdType.MESH
F32, BF16 = jnp.float32, jnp.bfloat16

beta_one = 0.9
beta_two = 0.95
bias_one = 1.0 - 0.9**10
bias_two = 1.0 - 0.95**10
epsilon = 1e-08

N = 1600
Q = 4
T = 16
SPLIT = [(0, 768), (768, 832)]
J = len(SPLIT)


def tiles(start, size):
    return [(j, min(256, start + size - j)) for j in range(start, start + size, 256)]


ROWS = dict(g=112, cf=128, A=64, B=128, C=48, D=48, E1=64, E2=64, F=64, G=128, H=112, Y=96, I=16)
KINDS = tuple(ROWS)
WHOLE = ("g", "cf", "G", "H", "Y", "I")

EARLY = (0, 1)


ORDER = [
    (0, "g", 0), (1, "g", 0), (0, "tr", 0), (0, "cf", 0), (2, "g", 0), (0, "m1", 0), (0, "m1", 1), (1, "cf", 0),
    (3, "g", 0), (0, "a", 0), (1, "m1", 1), (0, "a", 1), (2, "cf", 0), (0, "b", 0), (1, "a", 1), (1, "m1", 0),
    (2, "m1", 0), (0, "b", 1), (3, "cf", 0), (1, "b", 1), (2, "m1", 1), (1, "a", 0), (3, "m1", 0), (0, "ad", 0),
    (0, "ad", 1), (2, "a", 1), (2, "a", 0), (3, "m1", 1), (1, "b", 0), (0, "e", 0), (1, "ad", 1), (0, "e", 1),
    (2, "b", 1), (3, "a", 1), (1, "ad", 0), (2, "b", 0), (3, "a", 0), (0, "f", 0), (0, "f", 1), (2, "ad", 1),
    (1, "e", 1), (3, "b", 1), (2, "ad", 0), (1, "e", 0), (0, "m2", 0), (3, "b", 0), (1, "f", 1), (0, "m2", 1),
    (0, "gx", 0), (1, "f", 0), (2, "e", 1), (3, "ad", 1), (0, "h", 0), (1, "m2", 1), (2, "e", 0), (1, "m2", 0),
    (1, "gx", 0), (3, "ad", 0), (2, "f", 1), (2, "m2a", 1), (2, "f", 0), (1, "h", 0), (3, "e", 1), (2, "m2a", 0),
    (2, "ga", 0), (0, "i", 0), (2, "m2b", 1), (3, "e", 0), (2, "ha", 0), (3, "f", 1), (2, "m2b", 0), (2, "gb", 0),
    (3, "m2a", 1), (3, "f", 0), (0, "o", 0), (2, "hb", 0), (3, "m2a", 0), (3, "ga", 0), (1, "i", 0), (3, "m2b", 1),
    (3, "ha", 0), (3, "m2b", 0), (3, "gb", 0), (1, "o", 0), (3, "hb", 0), (2, "o", 0), (3, "o", 0),
]


def kernel(
    grad, basis, moment, second, nmv, nsv, dv,
    bv, bt, mv, sv, gath, part, part16, a_in, b_out, b_in, c_out, c_own, c_in, step, g_in, h_out, h_own, h_in, i_own, i_out, i_in,
    send, recv, recv_g, local,
):
    row, col = lax.axis_index("row"), lax.axis_index("col")
    core, zlo, y = row % 2, (row // 2) % 2, row // 4
    x, zhi = col % 4, col // 4

    def at_row(yy, zz, cc):
        return ((yy * 2 + zz) * 2 + cc, col)

    def at_col(zz, xx):
        return (row, zz * 4 + xx)

    x_up, x_down, x_far = (x + 1) % 4, (x + 3) % 4, (x + 2) % 4
    right, left = at_col(zhi, x_up), at_col(zhi, x_down)
    sibling = at_row(y, zlo, 1 - core)
    partner = at_row(y, 1 - zlo, core)
    peers_z = [at_col((zhi + d) % 4, x) for d in (1, 2, 3)]
    peers_y = [at_row((y + d) % 4, zlo, core) for d in (1, 2, 3)]
    peers_row = [partner] + [at_row((y + d) % 4, z, core) for d in (1, 2, 3) for z in (0, 1)]

    def ds(start, size):
        return pl.ds(pl.multiple_of(start, 16), size)

    def cols(j):
        return pl.ds(*SPLIT[j])

    def blk(dest):
        return (dest % 2 * 2 + dest // 2) * 64

    mine = (core * 2 + zlo) * 64 + y * T
    own = [
        pltpu.make_async_copy(grad.at[pl.ds(q * T, T)], gath.at[q, ds(mine, T)], local.at[q]) for q in range(Q)
    ]
    for c in own:
        c.start()
    load_b = pltpu.make_async_copy(basis, bv, local.at[4])
    load_m = pltpu.make_async_copy(moment, mv, local.at[5])
    load_s = pltpu.make_async_copy(second, sv, local.at[6])
    load_b.start()
    load_m.start()
    load_s.start()

    barrier = pltpu.get_barrier_semaphore()
    partners = [right, left, sibling] + peers_z + peers_row
    for d in partners:
        pl.semaphore_signal(barrier, inc=1, device_id=d, device_id_type=MESH)
    pl.semaphore_wait(barrier, len(partners))

    def put(kind, sem, src, dst, to):
        pltpu.make_async_remote_copy(
            src_ref=src, dst_ref=dst, send_sem=send.at[KINDS.index(kind)], recv_sem=sem, device_id=to,
            device_id_type=MESH,
        ).start()

    def arrival(kind, q, j=0):
        return recv.at[KINDS.index(kind), q, j]

    def await_rows(sem, ref):
        pltpu.make_async_copy(ref, ref, sem).wait()

    def got(kind, q, j=0):
        rows = ROWS[kind]
        span = part16.at[0, pl.ds(0, rows)]
        if kind not in WHOLE:
            span = part16.at[0, pl.ds(0, rows), cols(j)]
        await_rows(arrival(kind, q, j), span)

    def sent(kind):
        ref = part if kind == "G" else part16
        chunks = {"H": Q - len(EARLY), "Y": len(EARLY), "I": len(EARLY)}.get(kind, Q)
        span = ref.at[pl.ds(0, chunks), pl.ds(0, ROWS[kind])]
        await_rows(send.at[KINDS.index(kind)], span)

    def gather(q, j):
        own[q].wait()
        for d in peers_row:
            block = gath.at[q, ds(mine, T)]
            put("g", arrival("g", q), block, block, d)

    def gather_core(q, j):
        got("g", q)
        block = gath.at[q, ds(core * 128, 128)]
        put("cf", arrival("cf", q), block, block, sibling)

    def transpose(q, j):
        load_b.wait()
        for s, w in tiles(0, N):
            for c, v in tiles(0, N):
                bt[c : c + v, s : s + w] = bv[s : s + w, c : c + v].T

    seen = set()

    def first(*key):
        new = key not in seen
        seen.add(key)
        return new

    def multiply(q, j, rows):
        for s, w in tiles(*SPLIT[j]):
            p = jnp.dot(gath[q, rows], bv[:, s : s + w], preferred_element_type=F32)
            part[q, rows, s : s + w] = p
            part16[q, rows, s : s + w] = p.astype(BF16)

    def send_half(kind, q, j, block, ref, at, to):
        c = cols(j)
        put(kind, arrival(kind, q, j), part16.at[q, ds(block, 32), c], ref.at[q, pl.ds(at, 32), c], to)

    def send_far(q, j):
        send_half("A", q, j, blk(x_far), a_in, 0, right)
        send_half("A", q, j, blk(x_far) + 32, a_in, 32, left)

    def send_near(q, j):
        send_half("B", q, j, blk(x_up) + 32, b_in, 32, right)
        send_half("B", q, j, blk(x_down), b_in, 64, left)

    far_first = core == x % 2

    def forward_own(q, j):
        multiply(q, j, ds(core * 128, 128))
        pl.when(far_first)(lambda: send_far(q, j))
        pl.when(jnp.logical_not(far_first))(lambda: send_near(q, j))

    def forward_other(q, j):
        if first("m1", q):
            got("cf", q)
        multiply(q, j, ds((1 - core) * 128, 128))
        pl.when(far_first)(lambda: send_near(q, j))
        pl.when(jnp.logical_not(far_first))(lambda: send_far(q, j))

    def forward(q, j):
        if first("m1", q):
            got("cf", q)
        multiply(q, j, pl.ds(0, 256))
        send_far(q, j)
        send_near(q, j)

    def add_far(q, j):
        got("A", q, j)
        c = cols(j)
        for half, start in ((0, blk(x_up)), (1, blk(x_down) + 32)):
            for i in range(0, 32, T):
                at = half * 32 + i
                b_out[q, at : at + T, c] = (
                    part[q, ds(start + i, T), c] + a_in[q, at : at + T, c].astype(F32)
                ).astype(BF16)
        put("B", arrival("B", q, j), b_out.at[q, pl.ds(0, 32), c], b_in.at[q, pl.ds(0, 32), c], right)
        put("B", arrival("B", q, j), b_out.at[q, pl.ds(32, 32), c], b_in.at[q, pl.ds(96, 32), c], left)

    def add_x(q, j):
        got("B", q, j)
        c = cols(j)

        def total(i):
            return (
                part[q, ds(blk(x) + i, T), c] + b_in[q, ds(i, T), c].astype(F32) + b_in[q, ds(64 + i, T), c].astype(F32)
            )

        for i in range(0, 64, T):
            c_out[q, i : i + T, c] = total(i).astype(BF16)
        for d in (1, 2, 3):
            put(
                "C", arrival("C", q, j), c_out.at[q, ds((zhi + d) % 4 * T, T), c],
                c_in.at[q, pl.ds((d - 1) * T, T), c], peers_z[d - 1],
            )
        c_own[q, :, c] = total(zhi * T)

    def adam(q, j):
        if first("moments"):
            load_m.wait()
            load_s.wait()
        got("C", q, j)
        c = cols(j)
        rotated = c_own[q, :, c]
        for d in range(3):
            rotated += c_in[q, d * T : d * T + T, c].astype(F32)
        rows = pl.ds(q * T, T)
        nm = beta_one * mv[rows, c] + (1.0 - beta_one) * rotated
        ns = beta_two * sv[rows, c] + (1.0 - beta_two) * rotated * rotated
        nmv[rows, c] = nm
        nsv[rows, c] = ns
        block = step.at[q, ds(64 + zhi * T, T), c]
        block[...] = (nm / bias_one / (jnp.sqrt(ns / bias_two) + epsilon)).astype(BF16)
        for d in peers_z:
            put("D", arrival("D", q, j), block, block, d)

    def rows_of(q, j, start):
        return step.at[q, pl.ds(start, 32), cols(j)]

    def spread(q, j):
        got("D", q, j)
        put("E1", arrival("E1", q, j), rows_of(q, j, 64), rows_of(q, j, 0), right)
        put("E1", arrival("E1", q, j), rows_of(q, j, 96), rows_of(q, j, 160), left)
        put("E2", arrival("E2", q, j), rows_of(q, j, 96), rows_of(q, j, 32), right)
        put("E2", arrival("E2", q, j), rows_of(q, j, 64), rows_of(q, j, 128), left)

    def spread_far(q, j):
        got("E1", q, j)
        put("F", arrival("F", q, j), rows_of(q, j, 0), rows_of(q, j, 192), right)
        put("F", arrival("F", q, j), rows_of(q, j, 160), rows_of(q, j, 224), left)

    def back(q, j, start, size):
        rows = pl.ds(start, size)
        new = first("m2", q, start)
        for s, w in tiles(0, N):
            d = jnp.dot(step[q, rows, cols(j)], bt[cols(j), s : s + w], preferred_element_type=F32)
            if not new:
                d += part[q, rows, s : s + w]
            part[q, rows, s : s + w] = d

    def slot(dest):
        return (dest - x + 5) % 4 * 64

    def give_core(q, z):
        put(
            "G", recv_g.at[q, z], part.at[q, ds(slot(z * 2 + 1 - core), 64)], g_in.at[q, pl.ds(z * 64, 64)], sibling
        )

    def add_core(q, z):
        await_rows(recv_g.at[q, z], g_in.at[q, pl.ds(0, 64)])

        def total(yy):
            return part[q, ds(slot(z * 2 + core) + yy * T, T)] + g_in[q, ds(z * 64 + yy * T, T)]

        other = (z + zlo) % 2
        for d in range(4):
            yy = (y + d) % 4

            def pass_on(d=d, yy=yy):
                at = z * 64 + d * T
                h_out[q, ds(at, T)] = total(yy).astype(BF16)
                put(
                    "H", arrival("H", q), h_out.at[q, ds(at, T)], h_in.at[q, ds(other * 64 + d * T, T)],
                    at_row(yy, z, core),
                )

            if d:
                pass_on()
            else:
                pl.when(other == 1)(pass_on)

                @pl.when(other == 0)
                def _():
                    i_own[q] = total(y)

    def back_all(q, j):
        got("E2", q, j)
        got("F", q, j)
        back(q, j, 0, 256)

    def give_all(q, j):
        for z in (0, 1):
            give_core(q, z)

    def add_all(q, j):
        for z in (0, 1):
            await_rows(recv_g.at[q, z], g_in.at[q, pl.ds(0, 64)])

        def total(z, yy):
            return part[q, ds(slot(z * 2 + core) + yy * T, T)] + g_in[q, ds(z * 64 + yy * T, T)]

        for d in (1, 2, 3):
            yy = (y + d) % 4
            for z in (0, 1):
                at = d * 32 + z * T
                h_out[q, at : at + T] = total(z, yy).astype(BF16)
            put(
                "Y", arrival("Y", q), h_out.at[q, pl.ds(d * 32, 32)], h_in.at[q, pl.ds(d * 32, 32)], peers_y[d - 1]
            )
        for z in (0, 1):
            h_own[q, z * T : z * T + T] = total(z, y)

    def add_y(q, j):
        got("Y", q)

        def total(z):
            t = h_own[q, ds(z * T, T)]
            for d in (1, 2, 3):
                t += h_in[q, ds(d * 32 + z * T, T)].astype(F32)
            return t

        i_out[q] = total(1 - zlo).astype(BF16)
        put("I", arrival("I", q), i_out.at[q], i_in.at[q], partner)
        i_own[q] = total(zlo)

    def back_near(q, j):
        got("E2", q, j)
        back(q, j, 0, 192)

    def give_near(q, j):
        for z in (0, 1):
            pl.when(z * 2 + 1 - core != x_far)(lambda z=z: give_core(q, z))

    def add_near(q, j):
        for z in (0, 1):
            pl.when(z * 2 + core != x_far)(lambda z=z: add_core(q, z))

    def back_far(q, j):
        got("F", q, j)
        back(q, j, 192, 64)

    def give_far(q, j):
        for z in (0, 1):
            pl.when(z * 2 + 1 - core == x_far)(lambda z=z: give_core(q, z))

    def add_rest(q, j):
        for z in (0, 1):
            pl.when(z * 2 + core == x_far)(lambda z=z: add_core(q, z))

    def finish(q, j):
        total = i_own[q]
        if q in EARLY:
            got("I", q)
            total += i_in[q].astype(F32)
        else:
            got("H", q)
            for i in range(1, 8):
                total += h_in[q, i * T : i * T + T].astype(F32)
        dv[q * T : q * T + T] = total.astype(BF16)

    phases = dict(
        g=gather, cf=gather_core, tr=transpose, n=forward_own, mo=forward_other, m1=forward, a=add_far, b=add_x, ad=adam, e=spread, f=spread_far,
        m2=back_all, gx=give_all, h=add_all, i=add_y,
        m2a=back_near, ga=give_near, ha=add_near, m2b=back_far, gb=give_far, hb=add_rest, o=finish,
    )
    for q, name, j in ORDER:
        phases[name](q, j)
    for kind in KINDS:
        sent(kind)


def flush(a, b, c, out_a, out_b, out_c, sems):
    copies = [
        pltpu.make_async_copy(src, dst, sems.at[i])
        for i, (src, dst) in enumerate(((a, out_a), (b, out_b), (c, out_c)))
    ]
    for copy in copies:
        copy.start()
    for copy in copies:
        copy.wait()


def on_device(gradient, basis, moment, second):
    def vm(rows, dtype=BF16):
        return pltpu.VMEM((Q, rows, N), dtype)

    anywhere = pl.BlockSpec(memory_space=pl.ANY)
    in_vmem = pl.BlockSpec(memory_space=pltpu.VMEM)
    shapes = [((Q * T, N), F32), ((Q * T, N), F32), ((Q * T, N), BF16)]
    results = pl.pallas_call(
        kernel,
        out_shape=[pltpu.VMEM(*s) for s in shapes],
        in_specs=[anywhere] * 4,
        out_specs=[in_vmem] * 3,
        scratch_shapes=[pltpu.VMEM((N, N), BF16)] * 2 + [pltpu.VMEM((Q * T, N), F32)] * 2 + [
            vm(256), vm(256, F32), vm(256), vm(64), vm(64), vm(128), vm(64), vm(T, F32), vm(48), vm(256),
            vm(128, F32), vm(128), vm(32, F32), vm(128), vm(T, F32), vm(T), vm(T),
            pltpu.SemaphoreType.DMA((len(KINDS),)),
            pltpu.SemaphoreType.DMA((len(KINDS), Q, J)),
            pltpu.SemaphoreType.DMA((Q, 2)),
            pltpu.SemaphoreType.DMA((7,)),
        ],
        compiler_params=pltpu.CompilerParams(
            collective_id=0, has_side_effects=True, vmem_limit_bytes=56 * 1024 * 1024
        ),
        cost_estimate=pl.CostEstimate(flops=4 * 1024 * N * N, bytes_accessed=8 << 20, transcendentals=0),
        name="soap_step",
    )(gradient, basis, moment, second)
    return pl.pallas_call(
        flush,
        out_shape=[jax.ShapeDtypeStruct(*s) for s in shapes],
        in_specs=[anywhere] * 3,
        out_specs=[anywhere] * 3,
        scratch_shapes=[pltpu.SemaphoreType.DMA((3,))],
        compiler_params=pltpu.CompilerParams(vmem_limit_bytes=1024 * 1024),
        name="flush",
    )(*results)


def solution(mesh):
    return jax.shard_map(
        on_device,
        mesh=mesh,
        in_specs=(P("row", "col"), P("col", "row"), P("col", "row"), P("col", "row")),
        out_specs=(P("col", "row"), P("col", "row"), P("row", "col")),
        check_vma=False,
    )
```

```python
import jax
import jax.numpy as jnp
from jax import lax
from jax.experimental import pallas as pl
from jax.experimental.pallas import tpu as pltpu
from jax.sharding import PartitionSpec as P

MESH = pl.DeviceIdType.MESH
F32, BF16 = jnp.float32, jnp.bfloat16

beta_one = 0.9
beta_two = 0.95
bias_one = 1.0 - 0.9**10
bias_two = 1.0 - 0.95**10
epsilon = 1e-08

N = 1600
Q = 4
T = 16
SPLIT = [(0, 768), (768, 832)]
J = len(SPLIT)


def tiles(start, size):
    return [(j, min(256, start + size - j)) for j in range(start, start + size, 256)]


ROWS = dict(g=112, cf=128, A=64, B=128, C=48, D=48, E1=64, E2=64, F=64, G=128, H=112, Y=96, I=16)
KINDS = tuple(ROWS)
WHOLE = ("g", "cf", "G", "H", "Y", "I")

EARLY = (0, 1)


ORDER = [
    (0, "g", 0), (1, "g", 0), (0, "tr", 0), (0, "cf", 0), (2, "g", 0), (0, "m1", 0), (0, "m1", 1), (1, "cf", 0),
    (3, "g", 0), (0, "a", 0), (1, "m1", 1), (2, "cf", 0), (0, "a", 1), (1, "m1", 0), (0, "b", 0), (1, "a", 1),
    (2, "m1", 0), (3, "cf", 0), (0, "b", 1), (3, "m1", 1), (0, "ad", 0), (1, "a", 0), (1, "b", 1), (3, "m1", 0),
    (3, "a", 1), (0, "ad", 1), (2, "m1", 1), (1, "b", 0), (3, "a", 0), (1, "ad", 1), (3, "b", 1), (0, "e", 0),
    (0, "e", 1), (1, "ad", 0), (3, "b", 0), (0, "f", 0), (2, "a", 1), (0, "f", 1), (1, "e", 1), (2, "a", 0),
    (3, "ad", 1), (0, "m2", 0), (2, "b", 1), (1, "e", 0), (0, "m2", 1), (3, "ad", 0), (0, "gx", 0), (1, "f", 1),
    (2, "b", 0), (1, "f", 0), (3, "e", 1), (0, "h", 0), (2, "ad", 1), (1, "m2", 1), (3, "e", 0), (1, "m2", 0),
    (1, "gx", 0), (2, "ad", 0), (3, "f", 1), (3, "m2a", 1), (3, "f", 0), (1, "h", 0), (2, "e", 1), (3, "m2a", 0),
    (3, "ga", 0), (0, "i", 0), (3, "m2b", 1), (2, "e", 0), (3, "ha", 0), (3, "m2b", 0), (3, "gb", 0), (2, "f", 1),
    (2, "m2a", 1), (2, "f", 0), (3, "hb", 0), (2, "m2a", 0), (2, "ga", 0), (1, "i", 0), (2, "m2b", 1), (2, "ha", 0),
    (2, "m2b", 0), (2, "gb", 0), (2, "hb", 0), (0, "o", 0), (3, "o", 0), (1, "o", 0), (2, "o", 0),
]


def kernel(
    grad, basis, moment, second, nmv, nsv, dv,
    bv, bt, mv, sv, gath, part, part16, a_in, b_out, b_in, c_out, c_own, c_in, step, g_in, h_out, h_own, h_in, i_own, i_out, i_in,
    send, recv, recv_g, local,
):
    row, col = lax.axis_index("row"), lax.axis_index("col")
    core, zlo, y = row % 2, (row // 2) % 2, row // 4
    x, zhi = col % 4, col // 4

    def at_row(yy, zz, cc):
        return ((yy * 2 + zz) * 2 + cc, col)

    def at_col(zz, xx):
        return (row, zz * 4 + xx)

    x_up, x_down, x_far = (x + 1) % 4, (x + 3) % 4, (x + 2) % 4
    right, left = at_col(zhi, x_up), at_col(zhi, x_down)
    sibling = at_row(y, zlo, 1 - core)
    partner = at_row(y, 1 - zlo, core)
    peers_z = [at_col((zhi + d) % 4, x) for d in (1, 2, 3)]
    peers_y = [at_row((y + d) % 4, zlo, core) for d in (1, 2, 3)]
    peers_row = [partner] + [at_row((y + d) % 4, z, core) for d in (1, 2, 3) for z in (0, 1)]

    def ds(start, size):
        return pl.ds(pl.multiple_of(start, 16), size)

    def cols(j):
        return pl.ds(*SPLIT[j])

    def blk(dest):
        return (dest % 2 * 2 + dest // 2) * 64

    mine = (core * 2 + zlo) * 64 + y * T
    own = [
        pltpu.make_async_copy(grad.at[pl.ds(q * T, T)], gath.at[q, ds(mine, T)], local.at[q]) for q in range(Q)
    ]
    for c in own:
        c.start()
    load_b = pltpu.make_async_copy(basis, bv, local.at[4])
    load_m = pltpu.make_async_copy(moment, mv, local.at[5])
    load_s = pltpu.make_async_copy(second, sv, local.at[6])
    load_b.start()
    load_m.start()
    load_s.start()

    barrier = pltpu.get_barrier_semaphore()
    partners = [right, left, sibling] + peers_z + peers_row
    for d in partners:
        pl.semaphore_signal(barrier, inc=1, device_id=d, device_id_type=MESH)
    pl.semaphore_wait(barrier, len(partners))

    def put(kind, sem, src, dst, to):
        pltpu.make_async_remote_copy(
            src_ref=src, dst_ref=dst, send_sem=send.at[KINDS.index(kind)], recv_sem=sem, device_id=to,
            device_id_type=MESH,
        ).start()

    def arrival(kind, q, j=0):
        return recv.at[KINDS.index(kind), q, j]

    def await_rows(sem, ref):
        pltpu.make_async_copy(ref, ref, sem).wait()

    def got(kind, q, j=0):
        rows = ROWS[kind]
        span = part16.at[0, pl.ds(0, rows)]
        if kind not in WHOLE:
            span = part16.at[0, pl.ds(0, rows), cols(j)]
        await_rows(arrival(kind, q, j), span)

    def sent(kind):
        ref = part if kind == "G" else part16
        chunks = {"H": Q - len(EARLY), "Y": len(EARLY), "I": len(EARLY)}.get(kind, Q)
        span = ref.at[pl.ds(0, chunks), pl.ds(0, ROWS[kind])]
        await_rows(send.at[KINDS.index(kind)], span)

    def gather(q, j):
        own[q].wait()
        for d in peers_row:
            block = gath.at[q, ds(mine, T)]
            put("g", arrival("g", q), block, block, d)

    def gather_core(q, j):
        got("g", q)
        block = gath.at[q, ds(core * 128, 128)]
        put("cf", arrival("cf", q), block, block, sibling)

    def transpose(q, j):
        load_b.wait()
        for s, w in tiles(0, N):
            for c, v in tiles(0, N):
                bt[c : c + v, s : s + w] = bv[s : s + w, c : c + v].T

    seen = set()

    def first(*key):
        new = key not in seen
        seen.add(key)
        return new

    def multiply(q, j, rows):
        for s, w in tiles(*SPLIT[j]):
            p = jnp.dot(gath[q, rows], bv[:, s : s + w], preferred_element_type=F32)
            part[q, rows, s : s + w] = p
            part16[q, rows, s : s + w] = p.astype(BF16)

    def send_half(kind, q, j, block, ref, at, to):
        c = cols(j)
        put(kind, arrival(kind, q, j), part16.at[q, ds(block, 32), c], ref.at[q, pl.ds(at, 32), c], to)

    def send_far(q, j):
        send_half("A", q, j, blk(x_far), a_in, 0, right)
        send_half("A", q, j, blk(x_far) + 32, a_in, 32, left)

    def send_near(q, j):
        send_half("B", q, j, blk(x_up) + 32, b_in, 32, right)
        send_half("B", q, j, blk(x_down), b_in, 64, left)

    far_first = core == x % 2

    def forward_own(q, j):
        multiply(q, j, ds(core * 128, 128))
        pl.when(far_first)(lambda: send_far(q, j))
        pl.when(jnp.logical_not(far_first))(lambda: send_near(q, j))

    def forward_other(q, j):
        if first("m1", q):
            got("cf", q)
        multiply(q, j, ds((1 - core) * 128, 128))
        pl.when(far_first)(lambda: send_near(q, j))
        pl.when(jnp.logical_not(far_first))(lambda: send_far(q, j))

    def forward(q, j):
        if first("m1", q):
            got("cf", q)
        multiply(q, j, pl.ds(0, 256))
        send_far(q, j)
        send_near(q, j)

    def add_far(q, j):
        got("A", q, j)
        c = cols(j)
        for half, start in ((0, blk(x_up)), (1, blk(x_down) + 32)):
            for i in range(0, 32, T):
                at = half * 32 + i
                b_out[q, at : at + T, c] = (
                    part[q, ds(start + i, T), c] + a_in[q, at : at + T, c].astype(F32)
                ).astype(BF16)
        put("B", arrival("B", q, j), b_out.at[q, pl.ds(0, 32), c], b_in.at[q, pl.ds(0, 32), c], right)
        put("B", arrival("B", q, j), b_out.at[q, pl.ds(32, 32), c], b_in.at[q, pl.ds(96, 32), c], left)

    def add_x(q, j):
        got("B", q, j)
        c = cols(j)

        def total(i):
            return (
                part[q, ds(blk(x) + i, T), c] + b_in[q, ds(i, T), c].astype(F32) + b_in[q, ds(64 + i, T), c].astype(F32)
            )

        for i in range(0, 64, T):
            c_out[q, i : i + T, c] = total(i).astype(BF16)
        for d in (1, 2, 3):
            put(
                "C", arrival("C", q, j), c_out.at[q, ds((zhi + d) % 4 * T, T), c],
                c_in.at[q, pl.ds((d - 1) * T, T), c], peers_z[d - 1],
            )
        c_own[q, :, c] = total(zhi * T)

    def adam(q, j):
        if first("moments"):
            load_m.wait()
            load_s.wait()
        got("C", q, j)
        c = cols(j)
        rotated = c_own[q, :, c]
        for d in range(3):
            rotated += c_in[q, d * T : d * T + T, c].astype(F32)
        rows = pl.ds(q * T, T)
        nm = beta_one * mv[rows, c] + (1.0 - beta_one) * rotated
        ns = beta_two * sv[rows, c] + (1.0 - beta_two) * rotated * rotated
        nmv[rows, c] = nm
        nsv[rows, c] = ns
        block = step.at[q, ds(64 + zhi * T, T), c]
        block[...] = (nm / bias_one / (jnp.sqrt(ns / bias_two) + epsilon)).astype(BF16)
        for d in peers_z:
            put("D", arrival("D", q, j), block, block, d)

    def rows_of(q, j, start):
        return step.at[q, pl.ds(start, 32), cols(j)]

    def spread(q, j):
        got("D", q, j)
        put("E1", arrival("E1", q, j), rows_of(q, j, 64), rows_of(q, j, 0), right)
        put("E1", arrival("E1", q, j), rows_of(q, j, 96), rows_of(q, j, 160), left)
        put("E2", arrival("E2", q, j), rows_of(q, j, 96), rows_of(q, j, 32), right)
        put("E2", arrival("E2", q, j), rows_of(q, j, 64), rows_of(q, j, 128), left)

    def spread_far(q, j):
        got("E1", q, j)
        put("F", arrival("F", q, j), rows_of(q, j, 0), rows_of(q, j, 192), right)
        put("F", arrival("F", q, j), rows_of(q, j, 160), rows_of(q, j, 224), left)

    def back(q, j, start, size):
        rows = pl.ds(start, size)
        new = first("m2", q, start)
        for s, w in tiles(0, N):
            d = jnp.dot(step[q, rows, cols(j)], bt[cols(j), s : s + w], preferred_element_type=F32)
            if not new:
                d += part[q, rows, s : s + w]
            part[q, rows, s : s + w] = d

    def slot(dest):
        return (dest - x + 5) % 4 * 64

    def give_core(q, z):
        put(
            "G", recv_g.at[q, z], part.at[q, ds(slot(z * 2 + 1 - core), 64)], g_in.at[q, pl.ds(z * 64, 64)], sibling
        )

    def add_core(q, z):
        await_rows(recv_g.at[q, z], g_in.at[q, pl.ds(0, 64)])

        def total(yy):
            return part[q, ds(slot(z * 2 + core) + yy * T, T)] + g_in[q, ds(z * 64 + yy * T, T)]

        other = (z + zlo) % 2
        for d in range(4):
            yy = (y + d) % 4

            def pass_on(d=d, yy=yy):
                at = z * 64 + d * T
                h_out[q, ds(at, T)] = total(yy).astype(BF16)
                put(
                    "H", arrival("H", q), h_out.at[q, ds(at, T)], h_in.at[q, ds(other * 64 + d * T, T)],
                    at_row(yy, z, core),
                )

            if d:
                pass_on()
            else:
                pl.when(other == 1)(pass_on)

                @pl.when(other == 0)
                def _():
                    i_own[q] = total(y)

    def back_all(q, j):
        got("E2", q, j)
        got("F", q, j)
        back(q, j, 0, 256)

    def give_all(q, j):
        for z in (0, 1):
            give_core(q, z)

    def add_all(q, j):
        for z in (0, 1):
            await_rows(recv_g.at[q, z], g_in.at[q, pl.ds(0, 64)])

        def total(z, yy):
            return part[q, ds(slot(z * 2 + core) + yy * T, T)] + g_in[q, ds(z * 64 + yy * T, T)]

        for d in (1, 2, 3):
            yy = (y + d) % 4
            for z in (0, 1):
                at = d * 32 + z * T
                h_out[q, at : at + T] = total(z, yy).astype(BF16)
            put(
                "Y", arrival("Y", q), h_out.at[q, pl.ds(d * 32, 32)], h_in.at[q, pl.ds(d * 32, 32)], peers_y[d - 1]
            )
        for z in (0, 1):
            h_own[q, z * T : z * T + T] = total(z, y)

    def add_y(q, j):
        got("Y", q)

        def total(z):
            t = h_own[q, ds(z * T, T)]
            for d in (1, 2, 3):
                t += h_in[q, ds(d * 32 + z * T, T)].astype(F32)
            return t

        i_out[q] = total(1 - zlo).astype(BF16)
        put("I", arrival("I", q), i_out.at[q], i_in.at[q], partner)
        i_own[q] = total(zlo)

    def back_near(q, j):
        got("E2", q, j)
        back(q, j, 0, 192)

    def give_near(q, j):
        for z in (0, 1):
            pl.when(z * 2 + 1 - core != x_far)(lambda z=z: give_core(q, z))

    def add_near(q, j):
        for z in (0, 1):
            pl.when(z * 2 + core != x_far)(lambda z=z: add_core(q, z))

    def back_far(q, j):
        got("F", q, j)
        back(q, j, 192, 64)

    def give_far(q, j):
        for z in (0, 1):
            pl.when(z * 2 + 1 - core == x_far)(lambda z=z: give_core(q, z))

    def add_rest(q, j):
        for z in (0, 1):
            pl.when(z * 2 + core == x_far)(lambda z=z: add_core(q, z))

    def finish(q, j):
        total = i_own[q]
        if q in EARLY:
            got("I", q)
            total += i_in[q].astype(F32)
        else:
            got("H", q)
            for i in range(1, 8):
                total += h_in[q, i * T : i * T + T].astype(F32)
        dv[q * T : q * T + T] = total.astype(BF16)

    phases = dict(
        g=gather, cf=gather_core, tr=transpose, n=forward_own, mo=forward_other, m1=forward, a=add_far, b=add_x, ad=adam, e=spread, f=spread_far,
        m2=back_all, gx=give_all, h=add_all, i=add_y,
        m2a=back_near, ga=give_near, ha=add_near, m2b=back_far, gb=give_far, hb=add_rest, o=finish,
    )
    for q, name, j in ORDER:
        phases[name](q, j)
    for kind in KINDS:
        sent(kind)


def flush(a, b, c, out_a, out_b, out_c, sems):
    copies = [
        pltpu.make_async_copy(src, dst, sems.at[i])
        for i, (src, dst) in enumerate(((a, out_a), (b, out_b), (c, out_c)))
    ]
    for copy in copies:
        copy.start()
    for copy in copies:
        copy.wait()


def on_device(gradient, basis, moment, second):
    def vm(rows, dtype=BF16):
        return pltpu.VMEM((Q, rows, N), dtype)

    anywhere = pl.BlockSpec(memory_space=pl.ANY)
    in_vmem = pl.BlockSpec(memory_space=pltpu.VMEM)
    shapes = [((Q * T, N), F32), ((Q * T, N), F32), ((Q * T, N), BF16)]
    results = pl.pallas_call(
        kernel,
        out_shape=[pltpu.VMEM(*s) for s in shapes],
        in_specs=[anywhere] * 4,
        out_specs=[in_vmem] * 3,
        scratch_shapes=[pltpu.VMEM((N, N), BF16)] * 2 + [pltpu.VMEM((Q * T, N), F32)] * 2 + [
            vm(256), vm(256, F32), vm(256), vm(64), vm(64), vm(128), vm(64), vm(T, F32), vm(48), vm(256),
            vm(128, F32), vm(128), vm(32, F32), vm(128), vm(T, F32), vm(T), vm(T),
            pltpu.SemaphoreType.DMA((len(KINDS),)),
            pltpu.SemaphoreType.DMA((len(KINDS), Q, J)),
            pltpu.SemaphoreType.DMA((Q, 2)),
            pltpu.SemaphoreType.DMA((7,)),
        ],
        compiler_params=pltpu.CompilerParams(
            collective_id=0, has_side_effects=True, vmem_limit_bytes=56 * 1024 * 1024
        ),
        cost_estimate=pl.CostEstimate(flops=4 * 1024 * N * N, bytes_accessed=8 << 20, transcendentals=0),
        name="soap_step",
    )(gradient, basis, moment, second)
    return pl.pallas_call(
        flush,
        out_shape=[jax.ShapeDtypeStruct(*s) for s in shapes],
        in_specs=[anywhere] * 3,
        out_specs=[anywhere] * 3,
        scratch_shapes=[pltpu.SemaphoreType.DMA((3,))],
        compiler_params=pltpu.CompilerParams(vmem_limit_bytes=1024 * 1024),
        name="flush",
    )(*results)


def solution(mesh):
    return jax.shard_map(
        on_device,
        mesh=mesh,
        in_specs=(P("row", "col"), P("col", "row"), P("col", "row"), P("col", "row")),
        out_specs=(P("col", "row"), P("col", "row"), P("row", "col")),
        check_vma=False,
    )
```

```python
import jax
import jax.numpy as jnp
from jax import lax
from jax.experimental import pallas as pl
from jax.experimental.pallas import tpu as pltpu
from jax.sharding import PartitionSpec as P

MESH = pl.DeviceIdType.MESH
F32, BF16 = jnp.float32, jnp.bfloat16

beta_one = 0.9
beta_two = 0.95
bias_one = 1.0 - 0.9**10
bias_two = 1.0 - 0.95**10
epsilon = 1e-08

N = 1600
Q = 4
T = 16
SPLIT = [(0, 768), (768, 832)]
J = len(SPLIT)


def tiles(start, size):
    return [(j, min(256, start + size - j)) for j in range(start, start + size, 256)]


ROWS = dict(g=112, cf=128, A=64, B=128, C=48, D=48, E1=64, E2=64, F=64, G=128, H=112, S=16, Y=96, I=16)
KINDS = tuple(ROWS)
WHOLE = ("g", "cf", "G", "H", "S", "Y", "I")

EARLY = (0, 1)


ORDER = [
    (0, "g", 0), (1, "g", 0), (0, "tr", 0), (0, "cf", 0), (2, "g", 0), (0, "m1", 0), (0, "m1", 1), (1, "cf", 0),
    (3, "g", 0), (0, "a", 0), (1, "m1", 1), (2, "cf", 0), (0, "a", 1), (1, "m1", 0), (0, "b", 0), (1, "a", 1),
    (2, "m1", 0), (3, "cf", 0), (0, "b", 1), (3, "m1", 1), (0, "ad", 0), (1, "a", 0), (1, "b", 1), (3, "m1", 0),
    (3, "a", 1), (0, "ad", 1), (2, "m1", 1), (1, "b", 0), (3, "a", 0), (1, "ad", 1), (3, "b", 1), (0, "e", 0),
    (0, "e", 1), (1, "ad", 0), (3, "b", 0), (0, "f", 0), (2, "a", 1), (0, "f", 1), (1, "e", 1), (2, "a", 0),
    (3, "ad", 1), (0, "m2", 0), (2, "b", 1), (1, "e", 0), (0, "m2", 1), (3, "ad", 0), (0, "gx", 0), (1, "f", 1),
    (2, "b", 0), (1, "f", 0), (3, "e", 1), (0, "h", 0), (2, "ad", 1), (1, "m2", 1), (3, "e", 0), (1, "m2", 0),
    (1, "gx", 0), (2, "ad", 0), (3, "f", 1), (3, "m2a", 1), (3, "f", 0), (1, "h", 0), (2, "e", 1), (3, "m2a", 0),
    (3, "ga", 0), (0, "i", 0), (3, "m2b", 1), (2, "e", 0), (3, "ha", 0), (3, "m2b", 0), (3, "gb", 0), (2, "f", 1),
    (2, "m2a", 1), (2, "f", 0), (3, "hb", 0), (2, "m2a", 0), (2, "ga", 0), (1, "i", 0), (2, "m2b", 1), (2, "ha", 0),
    (2, "m2b", 0), (2, "gb", 0), (2, "hb", 0), (0, "o", 0), (3, "o", 0), (1, "o", 0), (2, "o", 0),
]


def kernel(
    grad, basis, moment, second, nmv, nsv, dv,
    bv, bt, mv, sv, gath, part, part16, a_in, b_out, b_in, c_out, c_own, c_in, step, g_in, h_out, h_own, h_in, i_own, i_out, i_in,
    send, recv, recv_g, local,
):
    row, col = lax.axis_index("row"), lax.axis_index("col")
    core, zlo, y = row % 2, (row // 2) % 2, row // 4
    x, zhi = col % 4, col // 4

    def at_row(yy, zz, cc):
        return ((yy * 2 + zz) * 2 + cc, col)

    def at_col(zz, xx):
        return (row, zz * 4 + xx)

    x_up, x_down, x_far = (x + 1) % 4, (x + 3) % 4, (x + 2) % 4
    right, left = at_col(zhi, x_up), at_col(zhi, x_down)
    sibling = at_row(y, zlo, 1 - core)
    partner = at_row(y, 1 - zlo, core)
    peers_z = [at_col((zhi + d) % 4, x) for d in (1, 2, 3)]
    peers_y = [at_row((y + d) % 4, zlo, core) for d in (1, 2, 3)]
    peers_row = [partner] + [at_row((y + d) % 4, z, core) for d in (1, 2, 3) for z in (0, 1)]

    def ds(start, size):
        return pl.ds(pl.multiple_of(start, 16), size)

    def cols(j):
        return pl.ds(*SPLIT[j])

    def blk(dest):
        return (dest % 2 * 2 + dest // 2) * 64

    mine = (core * 2 + zlo) * 64 + y * T
    own = [
        pltpu.make_async_copy(grad.at[pl.ds(q * T, T)], gath.at[q, ds(mine, T)], local.at[q]) for q in range(Q)
    ]
    for c in own:
        c.start()
    load_b = pltpu.make_async_copy(basis, bv, local.at[4])
    load_m = pltpu.make_async_copy(moment, mv, local.at[5])
    load_s = pltpu.make_async_copy(second, sv, local.at[6])
    load_b.start()
    load_m.start()
    load_s.start()

    barrier = pltpu.get_barrier_semaphore()
    partners = [right, left, sibling] + peers_z + peers_row
    for d in partners:
        pl.semaphore_signal(barrier, inc=1, device_id=d, device_id_type=MESH)
    pl.semaphore_wait(barrier, len(partners))

    def put(kind, sem, src, dst, to):
        pltpu.make_async_remote_copy(
            src_ref=src, dst_ref=dst, send_sem=send.at[KINDS.index(kind)], recv_sem=sem, device_id=to,
            device_id_type=MESH,
        ).start()

    def arrival(kind, q, j=0):
        return recv.at[KINDS.index(kind), q, j]

    def await_rows(sem, ref):
        pltpu.make_async_copy(ref, ref, sem).wait()

    def got(kind, q, j=0):
        rows = ROWS[kind]
        span = part16.at[0, pl.ds(0, rows)]
        if kind not in WHOLE:
            span = part16.at[0, pl.ds(0, rows), cols(j)]
        await_rows(arrival(kind, q, j), span)

    def sent(kind):
        ref = part if kind == "G" else part16
        chunks = {"H": Q - len(EARLY), "S": Q - len(EARLY), "Y": len(EARLY), "I": len(EARLY)}.get(kind, Q)

        def wait(rows):
            await_rows(send.at[KINDS.index(kind)], ref.at[pl.ds(0, chunks), pl.ds(0, rows)])

        if kind == "H":
            pl.when(y // 2 == core)(lambda: wait(96))
            pl.when(y // 2 != core)(lambda: wait(128))
        elif kind == "S":
            pl.when(y // 2 == core)(lambda: wait(T))
        else:
            wait(ROWS[kind])

    def gather(q, j):
        own[q].wait()
        for d in peers_row:
            block = gath.at[q, ds(mine, T)]
            put("g", arrival("g", q), block, block, d)

    def gather_core(q, j):
        got("g", q)
        block = gath.at[q, ds(core * 128, 128)]
        put("cf", arrival("cf", q), block, block, sibling)

    def transpose(q, j):
        load_b.wait()
        for s, w in tiles(0, N):
            for c, v in tiles(0, N):
                bt[c : c + v, s : s + w] = bv[s : s + w, c : c + v].T

    seen = set()

    def first(*key):
        new = key not in seen
        seen.add(key)
        return new

    def multiply(q, j, rows):
        for s, w in tiles(*SPLIT[j]):
            p = jnp.dot(gath[q, rows], bv[:, s : s + w], preferred_element_type=F32)
            part[q, rows, s : s + w] = p
            part16[q, rows, s : s + w] = p.astype(BF16)

    def send_half(kind, q, j, block, ref, at, to):
        c = cols(j)
        put(kind, arrival(kind, q, j), part16.at[q, ds(block, 32), c], ref.at[q, pl.ds(at, 32), c], to)

    def send_far(q, j):
        send_half("A", q, j, blk(x_far), a_in, 0, right)
        send_half("A", q, j, blk(x_far) + 32, a_in, 32, left)

    def send_near(q, j):
        send_half("B", q, j, blk(x_up) + 32, b_in, 32, right)
        send_half("B", q, j, blk(x_down), b_in, 64, left)

    far_first = core == x % 2

    def forward_own(q, j):
        multiply(q, j, ds(core * 128, 128))
        pl.when(far_first)(lambda: send_far(q, j))
        pl.when(jnp.logical_not(far_first))(lambda: send_near(q, j))

    def forward_other(q, j):
        if first("m1", q):
            got("cf", q)
        multiply(q, j, ds((1 - core) * 128, 128))
        pl.when(far_first)(lambda: send_near(q, j))
        pl.when(jnp.logical_not(far_first))(lambda: send_far(q, j))

    def forward(q, j):
        if first("m1", q):
            got("cf", q)
        multiply(q, j, pl.ds(0, 256))
        send_far(q, j)
        send_near(q, j)

    def add_far(q, j):
        got("A", q, j)
        c = cols(j)
        for half, start in ((0, blk(x_up)), (1, blk(x_down) + 32)):
            for i in range(0, 32, T):
                at = half * 32 + i
                b_out[q, at : at + T, c] = (
                    part[q, ds(start + i, T), c] + a_in[q, at : at + T, c].astype(F32)
                ).astype(BF16)
        put("B", arrival("B", q, j), b_out.at[q, pl.ds(0, 32), c], b_in.at[q, pl.ds(0, 32), c], right)
        put("B", arrival("B", q, j), b_out.at[q, pl.ds(32, 32), c], b_in.at[q, pl.ds(96, 32), c], left)

    def add_x(q, j):
        got("B", q, j)
        c = cols(j)

        def total(i):
            return (
                part[q, ds(blk(x) + i, T), c] + b_in[q, ds(i, T), c].astype(F32) + b_in[q, ds(64 + i, T), c].astype(F32)
            )

        for i in range(0, 64, T):
            c_out[q, i : i + T, c] = total(i).astype(BF16)
        for d in (1, 2, 3):
            put(
                "C", arrival("C", q, j), c_out.at[q, ds((zhi + d) % 4 * T, T), c],
                c_in.at[q, pl.ds((d - 1) * T, T), c], peers_z[d - 1],
            )
        c_own[q, :, c] = total(zhi * T)

    def adam(q, j):
        if first("moments"):
            load_m.wait()
            load_s.wait()
        got("C", q, j)
        c = cols(j)
        rotated = c_own[q, :, c]
        for d in range(3):
            rotated += c_in[q, d * T : d * T + T, c].astype(F32)
        rows = pl.ds(q * T, T)
        nm = beta_one * mv[rows, c] + (1.0 - beta_one) * rotated
        ns = beta_two * sv[rows, c] + (1.0 - beta_two) * rotated * rotated
        nmv[rows, c] = nm
        nsv[rows, c] = ns
        block = step.at[q, ds(64 + zhi * T, T), c]
        block[...] = (nm / bias_one / (jnp.sqrt(ns / bias_two) + epsilon)).astype(BF16)
        for d in peers_z:
            put("D", arrival("D", q, j), block, block, d)

    def rows_of(q, j, start):
        return step.at[q, pl.ds(start, 32), cols(j)]

    def spread(q, j):
        got("D", q, j)
        put("E1", arrival("E1", q, j), rows_of(q, j, 64), rows_of(q, j, 0), right)
        put("E1", arrival("E1", q, j), rows_of(q, j, 96), rows_of(q, j, 160), left)
        put("E2", arrival("E2", q, j), rows_of(q, j, 96), rows_of(q, j, 32), right)
        put("E2", arrival("E2", q, j), rows_of(q, j, 64), rows_of(q, j, 128), left)

    def spread_far(q, j):
        got("E1", q, j)
        put("F", arrival("F", q, j), rows_of(q, j, 0), rows_of(q, j, 192), right)
        put("F", arrival("F", q, j), rows_of(q, j, 160), rows_of(q, j, 224), left)

    def back(q, j, start, size):
        rows = pl.ds(start, size)
        new = first("m2", q, start)
        for s, w in tiles(0, N):
            d = jnp.dot(step[q, rows, cols(j)], bt[cols(j), s : s + w], preferred_element_type=F32)
            if not new:
                d += part[q, rows, s : s + w]
            part[q, rows, s : s + w] = d

    def slot(dest):
        return (dest - x + 5) % 4 * 64

    def give_core(q, z):
        put(
            "G", recv_g.at[q, z], part.at[q, ds(slot(z * 2 + 1 - core), 64)], g_in.at[q, pl.ds(z * 64, 64)], sibling
        )

    def give_half(q, block):
        put(
            "G", recv_g.at[q, block], part.at[q, ds(block * 64 + (1 - core) * 32, 32)],
            g_in.at[q, pl.ds(block * 32, 32)], sibling,
        )

    def add_half(q, block):
        await_rows(recv_g.at[q, block], g_in.at[q, pl.ds(0, 32)])
        dest = (x + block + 3) % 4
        z, c = dest // 2, dest % 2
        other = (z + zlo) % 2
        for i in (0, 1):
            yy = core * 2 + i
            d = (yy + 4 - y) % 4
            at = block * 32 + i * T
            total = part[q, ds(block * 64 + core * 32 + i * T, T)] + g_in[q, at : at + T]
            h_out[q, at : at + T] = total.astype(BF16)
            here = jnp.logical_and(d == 0, other == 0)

            @pl.when(jnp.logical_not(here))
            def _(at=at, yy=yy, d=d):
                put(
                    "H", arrival("H", q), h_out.at[q, pl.ds(at, T)], h_in.at[q, ds(other * 64 + d * T, T)],
                    at_row(yy, z, c),
                )

            @pl.when(jnp.logical_and(here, c != core))
            def _(at=at):
                put("S", arrival("S", q), h_out.at[q, pl.ds(at, T)], h_in.at[q, pl.ds(0, T)], sibling)

            @pl.when(jnp.logical_and(here, c == core))
            def _(total=total):
                i_own[q] = total

    def back_all(q, j):
        got("E2", q, j)
        got("F", q, j)
        back(q, j, 0, 256)

    def give_all(q, j):
        for z in (0, 1):
            give_core(q, z)

    def add_all(q, j):
        for z in (0, 1):
            await_rows(recv_g.at[q, z], g_in.at[q, pl.ds(0, 64)])

        def total(z, yy):
            return part[q, ds(slot(z * 2 + core) + yy * T, T)] + g_in[q, ds(z * 64 + yy * T, T)]

        for d in (1, 2, 3):
            yy = (y + d) % 4
            for z in (0, 1):
                at = d * 32 + z * T
                h_out[q, at : at + T] = total(z, yy).astype(BF16)
            put(
                "Y", arrival("Y", q), h_out.at[q, pl.ds(d * 32, 32)], h_in.at[q, pl.ds(d * 32, 32)], peers_y[d - 1]
            )
        for z in (0, 1):
            h_own[q, z * T : z * T + T] = total(z, y)

    def add_y(q, j):
        got("Y", q)

        def total(z):
            t = h_own[q, ds(z * T, T)]
            for d in (1, 2, 3):
                t += h_in[q, ds(d * 32 + z * T, T)].astype(F32)
            return t

        i_out[q] = total(1 - zlo).astype(BF16)
        put("I", arrival("I", q), i_out.at[q], i_in.at[q], partner)
        i_own[q] = total(zlo)

    def back_near(q, j):
        got("E2", q, j)
        back(q, j, 0, 192)

    def give_near(q, j):
        for block in (0, 1, 2):
            give_half(q, block)

    def add_near(q, j):
        for block in (0, 1, 2):
            add_half(q, block)

    def back_far(q, j):
        got("F", q, j)
        back(q, j, 192, 64)

    def give_far(q, j):
        give_half(q, 3)

    def add_rest(q, j):
        add_half(q, 3)

    def finish(q, j):
        if q in EARLY:
            got("I", q)
            total = i_own[q] + i_in[q].astype(F32)
        else:

            @pl.when(y // 2 != core)
            def _():
                got("S", q)
                i_own[q] = h_in[q, pl.ds(0, T)].astype(F32)

            got("H", q)
            total = i_own[q]
            for i in range(1, 8):
                total += h_in[q, i * T : i * T + T].astype(F32)
        dv[q * T : q * T + T] = total.astype(BF16)

    phases = dict(
        g=gather, cf=gather_core, tr=transpose, n=forward_own, mo=forward_other, m1=forward, a=add_far, b=add_x, ad=adam, e=spread, f=spread_far,
        m2=back_all, gx=give_all, h=add_all, i=add_y,
        m2a=back_near, ga=give_near, ha=add_near, m2b=back_far, gb=give_far, hb=add_rest, o=finish,
    )
    for q, name, j in ORDER:
        phases[name](q, j)
    for kind in KINDS:
        sent(kind)


def flush(a, b, c, out_a, out_b, out_c, sems):
    copies = [
        pltpu.make_async_copy(src, dst, sems.at[i])
        for i, (src, dst) in enumerate(((a, out_a), (b, out_b), (c, out_c)))
    ]
    for copy in copies:
        copy.start()
    for copy in copies:
        copy.wait()


def on_device(gradient, basis, moment, second):
    def vm(rows, dtype=BF16):
        return pltpu.VMEM((Q, rows, N), dtype)

    anywhere = pl.BlockSpec(memory_space=pl.ANY)
    in_vmem = pl.BlockSpec(memory_space=pltpu.VMEM)
    shapes = [((Q * T, N), F32), ((Q * T, N), F32), ((Q * T, N), BF16)]
    results = pl.pallas_call(
        kernel,
        out_shape=[pltpu.VMEM(*s) for s in shapes],
        in_specs=[anywhere] * 4,
        out_specs=[in_vmem] * 3,
        scratch_shapes=[pltpu.VMEM((N, N), BF16)] * 2 + [pltpu.VMEM((Q * T, N), F32)] * 2 + [
            vm(256), vm(256, F32), vm(256), vm(64), vm(64), vm(128), vm(64), vm(T, F32), vm(48), vm(256),
            vm(128, F32), vm(128), vm(32, F32), vm(128), vm(T, F32), vm(T), vm(T),
            pltpu.SemaphoreType.DMA((len(KINDS),)),
            pltpu.SemaphoreType.DMA((len(KINDS), Q, J)),
            pltpu.SemaphoreType.DMA((Q, 4)),
            pltpu.SemaphoreType.DMA((7,)),
        ],
        compiler_params=pltpu.CompilerParams(
            collective_id=0, has_side_effects=True, vmem_limit_bytes=56 * 1024 * 1024
        ),
        cost_estimate=pl.CostEstimate(flops=4 * 1024 * N * N, bytes_accessed=8 << 20, transcendentals=0),
        name="soap_step",
    )(gradient, basis, moment, second)
    return pl.pallas_call(
        flush,
        out_shape=[jax.ShapeDtypeStruct(*s) for s in shapes],
        in_specs=[anywhere] * 3,
        out_specs=[anywhere] * 3,
        scratch_shapes=[pltpu.SemaphoreType.DMA((3,))],
        compiler_params=pltpu.CompilerParams(vmem_limit_bytes=1024 * 1024),
        name="flush",
    )(*results)


def solution(mesh):
    return jax.shard_map(
        on_device,
        mesh=mesh,
        in_specs=(P("row", "col"), P("col", "row"), P("col", "row"), P("col", "row")),
        out_specs=(P("col", "row"), P("col", "row"), P("row", "col")),
        check_vma=False,
    )
```
